32 devices in a mesh: group: 2 (over x), seq: 8 (over z, y), res: 2 (over core).
Axes of the slice: x: 2, y: 2, z: 4, core: 2. Of those that a mesh axis runs over, the one named last changes fastest.
Arguments:
- alignment: bfloat16 [1024, 128, 256], P(('group', 'seq'), 'res'), parts along dimension 0, may hold values from -8 to 8
- ln_gain: float32 [256], replicated, may hold values from 0.5 to 1.5
- ln_bias: float32 [256], replicated, may hold values from -0.6 to 0.6
- w_left: bfloat16 [256, 32], replicated, may hold values from -0.375 to 0.375
- bias_left: float32 [32], replicated, may hold values from -0.6 to 0.6
- w_right: bfloat16 [256, 32], replicated, may hold values from -0.375 to 0.375
- bias_right: float32 [32], replicated, may hold values from -0.6 to 0.6
- w_out: bfloat16 [1024, 128], replicated, may hold values from -1.5 to 1.5
- bias_out: float32 [128], replicated, may hold values from -0.5 to 0.5
Outputs:
- pair_update: bfloat16 [256, 128, 128], P(('group', 'seq'), 'res'), parts along dimension 0
The draws below stay inside these ranges and needn't reach their ends.
There are 2 independent parts, one for each index of `group`. The reference program is written for one: setup_inputs(seed, part) draws one part's arguments, and reference() takes and returns one part's arrays. A program takes and returns all parts, laid end to end along the dimension named above; an argument that names none is the same for every part. Nothing has to cross between parts.
All inputs are finite; a program needn't handle non-finite values.
Results may differ from the reference program's by a relative error of at most 0.0034.
Values may be sent and summed in bfloat16 or wider, within the bound.
A program may use at most 64 MiB of HBM per device.

```python
import math
import jax
import jax.numpy as jnp
from jax import lax

C = 256
PROJ = 32
OUT = 128
S_DEV = 64
S = 512
L = 128
N_SEQ = 8


def draw_alignment(key, part):
    factor_count = 16
    subkeys = jax.random.split(jax.random.fold_in(key, 11), 3)
    jitter = jax.random.normal(subkeys[0], (S, L, C), jnp.float32)
    loadings = jax.random.normal(subkeys[1], (S, factor_count), jnp.float32)
    shapes = jax.random.normal(subkeys[2], (factor_count, L * C), jnp.float32) / math.sqrt(factor_count)
    shared = jnp.dot(loadings, shapes, precision=lax.Precision.HIGHEST).reshape(S, L, C)
    return jnp.clip(jitter + shared, -8.0, 8.0).astype(jnp.bfloat16)


def gaussian(key, extent, scale, most, dtype=jnp.bfloat16):
    result = jax.random.normal(key, extent, jnp.float32) * scale
    return jnp.minimum(jnp.maximum(result, -most), most).astype(dtype)


def setup_inputs(seed: int = 0, part: int = 0) -> dict:
    keys = jax.random.split(jax.random.key(seed), 10)
    part_splits = jax.random.split(jax.random.fold_in(keys[9], part), 10)
    alignment = draw_alignment(jax.random.fold_in(jax.random.fold_in(keys[9], part), 71), part)
    ln_gain = jnp.clip(jax.random.uniform(keys[1], (C,), jnp.float32, 0.5, 1.5), 0.5, 1.5)
    ln_bias = gaussian(keys[2], (C,), 0.15, 0.6, jnp.float32)
    w_left = gaussian(keys[3], (C, PROJ), C ** -0.5, 0.375)
    bias_left = gaussian(keys[4], (PROJ,), 0.15, 0.6, jnp.float32)
    w_right = gaussian(keys[5], (C, PROJ), C ** -0.5, 0.375)
    bias_right = gaussian(keys[6], (PROJ,), 0.15, 0.6, jnp.float32)
    w_out = gaussian(keys[7], (PROJ * PROJ, OUT), (max(1, PROJ * PROJ // 64)) ** -0.5, 1.5)
    bias_out = jnp.clip(jax.random.uniform(keys[8], (OUT,), jnp.float32, -0.5, 0.5), -0.5, 0.5)
    return dict(alignment=alignment, ln_gain=ln_gain, ln_bias=ln_bias, w_left=w_left, bias_left=bias_left, w_right=w_right, bias_right=bias_right, w_out=w_out, bias_out=bias_out)


def normalize(alignment, ln_gain, ln_bias):
    values = alignment.astype(jnp.float32)
    center = lax.optimization_barrier(jnp.mean(values, axis=-1, keepdims=True))
    spread = lax.optimization_barrier(jnp.mean(jnp.square(values - center), axis=-1, keepdims=True))
    return ((values - center) * lax.rsqrt(spread + 1e-05) * ln_gain + ln_bias).astype(jnp.bfloat16)

def project(normed, weight, offset):
    flattened = normed.reshape(-1, normed.shape[-1])
    return (jnp.dot(flattened, weight, preferred_element_type=jnp.float32) + offset).astype(jnp.bfloat16)

def reference(alignment, ln_gain, ln_bias, w_left, bias_left, w_right, bias_right, w_out, bias_out):
    normed = normalize(alignment, ln_gain, ln_bias)
    left_groups = project(normed, w_left, bias_left).reshape(N_SEQ, S_DEV, L, PROJ)
    right_groups = project(normed, w_right, bias_right).reshape(N_SEQ, S_DEV, L, PROJ)
    weight_cube = w_out.astype(jnp.float32).reshape(PROJ, PROJ, OUT)
    height = math.gcd(L, 32)

    def group_step(summed, operands):
        left_group, right_group = operands
        right_wide = right_group.astype(jnp.float32)
        left_blocks = left_group.reshape(S_DEV, L // height, height, PROJ).transpose(1, 0, 2, 3)

        def block_term(left_block):
            outers = jnp.einsum('sic,sje->icej', left_block.astype(jnp.float32), right_wide)
            outers = lax.optimization_barrier(outers.astype(jnp.bfloat16)).astype(jnp.float32)
            return jnp.einsum('icej,ceo->ijo', outers, weight_cube)
        pieces = lax.map(block_term, left_blocks).reshape(L, L, OUT)
        return (summed + pieces, None)
    summed, unused = lax.scan(group_step, jnp.zeros((L, L, OUT), jnp.float32), (left_groups, right_groups))
    return (summed / S + bias_out).astype(jnp.bfloat16)
```

```python
import functools
import math

import jax
import jax.numpy as jnp
from jax import lax
from jax.experimental import pallas as pl
from jax.experimental.pallas import tpu as pltpu
from jax.sharding import PartitionSpec as P

MESH = pl.DeviceIdType.MESH
LANES = 128


def normalize(alignment, ln_gain, ln_bias):
    values = alignment.astype(jnp.float32)
    center = jnp.mean(values, axis=-1, keepdims=True)
    spread = jnp.mean(jnp.square(values - center), axis=-1, keepdims=True)
    return ((values - center) * lax.rsqrt(spread + 1e-05) * ln_gain + ln_bias).astype(jnp.bfloat16)


def project(normed, weight, offset):
    flattened = normed.reshape(-1, normed.shape[-1])
    return (jnp.dot(flattened, weight, preferred_element_type=jnp.float32) + offset).astype(
        jnp.bfloat16
    )


def pair_tile(left_rows, right_rows, weight_cube, rows_here):
    sequences = left_rows.shape[0]
    proj_width = weight_cube.shape[0]
    height = math.gcd(rows_here, 16)
    left_blocks = left_rows.reshape(sequences, rows_here // height, height, proj_width).transpose(
        1, 0, 2, 3
    )
    right_cube = right_rows.reshape(sequences, -1, proj_width)

    def one_block(left_block):
        outers = jnp.einsum(
            "sic,sje->icej", left_block, right_cube, preferred_element_type=jnp.float32
        ).astype(jnp.bfloat16)
        return jnp.einsum("icej,ceo->ijo", outers, weight_cube, preferred_element_type=jnp.float32)

    pieces = lax.map(one_block, left_blocks)
    return pieces.reshape(rows_here, right_cube.shape[1], weight_cube.shape[2])


def plain(alignment, ln_gain, ln_bias, w_left, bias_left, w_right, bias_right, w_out, bias_out):
    sequences = alignment.shape[0]
    residues = alignment.shape[1]
    proj_width = w_left.shape[1]
    out_width = w_out.shape[1]
    normed = normalize(alignment, ln_gain, ln_bias)
    left_rows = project(normed, w_left, bias_left).reshape(sequences, residues * proj_width)
    right_rows = project(normed, w_right, bias_right).reshape(sequences, residues * proj_width)
    weight_cube = w_out.reshape(proj_width, proj_width, out_width)
    columns = lax.all_gather(left_rows, "res", axis=1, tiled=True)
    width_all = columns.shape[1] // proj_width
    devices_seq = lax.axis_size("seq")
    kept_rows = width_all // devices_seq
    summed = lax.psum_scatter(
        pair_tile(columns, right_rows, weight_cube, lax.axis_size("seq") * kept_rows),
        "seq",
        scatter_dimension=0,
        tiled=True,
    )
    return (summed / (sequences * devices_seq) + bias_out).astype(jnp.bfloat16)


def fused_kernel(
    dims,
    a_hbm, gain_ref, beta_ref, wl_ref, bl_ref, wr_ref, br_ref, w_ref, bo_ref,
    out_ref,
    a_buf, w_tiled, proj_l, proj_r, l_send, l_all, r_all, lt_f32, lt, outer, lhs, outs,
    load_sem, r_recv, up_sem, down_sem, side_sem, l_send_sem, l_recv, core_send,
):
    n_seq, n_res, depth, s_dev, block, chunks, width, channels, proj = dims
    pack = LANES // proj
    quads = block // pack
    total = n_seq * s_dev
    p = lax.axis_index("seq")
    r = lax.axis_index("res")
    rows = n_seq // depth
    z = p // depth
    y = p % depth
    side = z * depth + (depth - 1 - y)

    loads = []
    for k in range(chunks):
        load = pltpu.make_async_copy(
            a_hbm.at[:, pl.ds(k * block, block), :], a_buf.at[k], load_sem.at[k]
        )
        load.start()
        loads.append(load)

    barrier = pltpu.get_barrier_semaphore()
    for d in range(1, n_seq):
        pl.semaphore_signal(
            barrier, inc=1, device_id={"seq": lax.rem(p + d, n_seq)}, device_id_type=MESH
        )
    pl.semaphore_signal(barrier, inc=1, device_id={"res": 1 - r}, device_id_type=MESH)

    def tile4(v):
        return jnp.concatenate([v] * pack, axis=1)

    w_tiled[:, :LANES] = tile4(wl_ref[...].astype(jnp.float32)).astype(jnp.bfloat16)
    w_tiled[:, LANES:] = tile4(wr_ref[...].astype(jnp.float32)).astype(jnp.bfloat16)
    bias_l = tile4(bl_ref[...])
    bias_r = tile4(br_ref[...])
    gain = gain_ref[...]
    beta = beta_ref[...]
    lane = lax.broadcasted_iota(jnp.int32, (s_dev, LANES), 1) // proj

    def copy_r(k, slot, sem, target):
        return pltpu.make_async_remote_copy(
            src_ref=r_all.at[k, slot],
            dst_ref=r_all.at[k, slot],
            send_sem=sem.at[k, slot],
            recv_sem=r_recv.at[k, slot],
            device_id={"seq": target},
            device_id_type=MESH,
        )

    def copy_up(k, slot):
        return copy_r(k, slot, up_sem, p + depth)

    def copy_down(k, slot):
        return copy_r(k, slot, down_sem, p - depth)

    def copy_side(k, slot):
        return copy_r(k, slot, side_sem, side)

    def copy_l(k):
        return pltpu.make_async_remote_copy(
            src_ref=l_send.at[k],
            dst_ref=l_all.at[p],
            send_sem=l_send_sem.at[k],
            recv_sem=l_recv.at[p],
            device_id={"seq": r * chunks + k},
            device_id_type=MESH,
        )

    def copy_core(slot):
        return pltpu.make_async_remote_copy(
            src_ref=l_all.at[slot],
            dst_ref=l_all.at[slot],
            send_sem=core_send.at[slot],
            recv_sem=l_recv.at[slot],
            device_id={"res": 1 - r},
            device_id_type=MESH,
        )

    seqs = 16
    for k in range(chunks):
        loads[k].wait()

        def norm_step(t, carry, k=k):
            values = a_buf[k, pl.ds(t * seqs, seqs)].reshape(seqs * block, channels)
            values = values.astype(jnp.float32)
            center = jnp.mean(values, axis=-1, keepdims=True)
            values = values - center
            spread = jnp.mean(jnp.square(values), axis=-1, keepdims=True)
            normed = (values * lax.rsqrt(spread + 1e-05) * gain + beta).astype(jnp.bfloat16)
            result = jnp.dot(normed, w_tiled[...], preferred_element_type=jnp.float32)
            here = pl.ds(t * (seqs * block), seqs * block)
            proj_l[here, :] = result[:, :LANES] + bias_l
            proj_r[here, :] = result[:, LANES:] + bias_r
            return carry

        lax.fori_loop(0, s_dev // seqs, norm_step, 0)

        for q in range(quads):
            columns = slice(q * LANES, (q + 1) * LANES)

            def merge(ref):
                merged = ref[pl.ds(q * pack, s_dev, stride=block), :]
                for m in range(1, pack):
                    merged = jnp.where(
                        lane == m, ref[pl.ds(q * pack + m, s_dev, stride=block), :], merged
                    )
                return merged.astype(jnp.bfloat16)

            r_all[k, p, :, columns] = merge(proj_r)
            l_send[k, :, columns] = merge(proj_l)

        if k == 0:
            pl.semaphore_wait(barrier, n_seq)

        @pl.when(z + 1 < rows)
        def _():
            copy_up(k, p).start()

        @pl.when(z > 0)
        def _():
            copy_down(k, p).start()

        copy_side(k, p).start()

        @pl.when(r * chunks + k != p)
        def _():
            copy_l(k).start()

        @pl.when(r * chunks + k == p)
        def _():
            l_all[p] = l_send[k]

    def forward(k):
        for d in range(1, rows):
            @pl.when(z - d >= 0)
            def _():
                slot = p - d * depth
                copy_down(k, slot).wait_recv()
                copy_side(k, slot).start()

                @pl.when(z + 1 < rows)
                def _():
                    copy_up(k, slot).start()

            @pl.when(z + d < rows)
            def _():
                slot = p + d * depth
                copy_down(k, slot).wait_recv()
                copy_side(k, slot).start()

                @pl.when(z > 0)
                def _():
                    copy_down(k, slot).start()

    def gather_left():
        owner = p // chunks == r
        for d in range(n_seq):
            slot = lax.rem(p + d, n_seq)

            @pl.when(owner)
            def _():
                if d > 0:
                    copy_core(slot).wait_recv()
                copy_core(slot).start()

            @pl.when(jnp.logical_not(owner))
            def _():
                copy_core(slot).wait_recv()

        left = l_all[...].reshape(total, block * proj)
        for t in range(total // LANES):
            lt_f32[t] = jnp.transpose(left[t * LANES : (t + 1) * LANES].astype(jnp.float32))
            for c in range(proj):
                lt[c * block : (c + 1) * block, t * LANES : (t + 1) * LANES] = lt_f32[
                    t, pl.ds(c, block, stride=proj), :
                ].astype(jnp.bfloat16)

    high = (lax.broadcasted_iota(jnp.int32, (block, LANES), 1) // (2 * proj)) == 1
    odd = ((lax.broadcasted_iota(jnp.int32, (block, LANES), 1) // proj) % 2) == 1

    def compute(k):
        for zz in range(rows):
            copy_side(k, zz * depth + (depth - 1 - y)).wait_recv()
        right = r_all[k].reshape(total, block * proj)
        outer[...] = jnp.dot(lt[...], right, preferred_element_type=jnp.float32)

        def regroup(cq, carry):
            for jq in range(quads):
                v = [
                    outer[pl.ds((cq * pack + m) * block, block), jq * LANES : (jq + 1) * LANES]
                    for m in range(pack)
                ]
                a0 = jnp.where(high, pltpu.roll(v[2], 2 * proj, 1), v[0])
                a2 = jnp.where(high, v[2], pltpu.roll(v[0], 2 * proj, 1))
                a1 = jnp.where(high, pltpu.roll(v[3], 2 * proj, 1), v[1])
                a3 = jnp.where(high, v[3], pltpu.roll(v[1], 2 * proj, 1))
                t = [
                    jnp.where(odd, pltpu.roll(a1, proj, 1), a0),
                    jnp.where(odd, a1, pltpu.roll(a0, 3 * proj, 1)),
                    jnp.where(odd, pltpu.roll(a3, proj, 1), a2),
                    jnp.where(odd, a3, pltpu.roll(a2, 3 * proj, 1)),
                ]
                for m in range(pack):
                    lhs[
                        (jq * pack + m) * block : (jq * pack + m + 1) * block,
                        pl.ds(pl.multiple_of(cq * LANES, LANES), LANES),
                    ] = t[m].astype(jnp.bfloat16)
            return carry

        lax.fori_loop(0, proj // pack, regroup, 0)
        outs[...] = (
            jnp.dot(lhs[...], w_ref[...], preferred_element_type=jnp.float32) * (1.0 / total)
            + bo_ref[...]
        )
        for i in range(block):
            out_ref[i, pl.ds(k * block, block), :] = outs[
                pl.ds(i, block, stride=block), :
            ].astype(jnp.bfloat16)

    forward(0)
    gather_left()
    for k in range(chunks):
        if k + 1 < chunks:
            forward(k + 1)
        compute(k)

    owner = p // chunks == r
    for k in range(chunks):
        @pl.when(r * chunks + k != p)
        def _():
            copy_l(k).wait_send()

        for zz in range(rows):
            slot = zz * depth + y
            copy_side(k, slot).wait_send()

            @pl.when(jnp.logical_and(zz <= z, z + 1 < rows))
            def _():
                copy_up(k, slot).wait_send()

            @pl.when(jnp.logical_and(zz >= z, z > 0))
            def _():
                copy_down(k, slot).wait_send()

    @pl.when(owner)
    def _():
        for slot in range(n_seq):
            copy_core(slot).wait_send()


def shards(n_seq, n_res, alignment, ln_gain, ln_bias, w_left, bias_left, w_right, bias_right, w_out, bias_out):
    s_dev, width, channels = alignment.shape
    proj = w_left.shape[1]
    out_width = w_out.shape[1]
    block = width * n_res // n_seq
    depth = 2
    fits = (
        n_res == 2
        and n_seq % depth == 0
        and block % 16 == 0
        and width % block == 0
        and proj * 4 == LANES
        and out_width == LANES
        and s_dev % 16 == 0
        and (n_seq * s_dev) % LANES == 0
    )
    if not fits:
        return plain(
            alignment, ln_gain, ln_bias, w_left, bias_left, w_right, bias_right, w_out, bias_out
        )
    chunks = width // block
    total = n_seq * s_dev
    dims = (n_seq, n_res, depth, s_dev, block, chunks, width, channels, proj)
    vmem = pl.BlockSpec(memory_space=pltpu.VMEM)
    wide = block * proj
    return pl.pallas_call(
        functools.partial(fused_kernel, dims),
        out_shape=jax.ShapeDtypeStruct((block, width, out_width), jnp.bfloat16),
        in_specs=[pl.BlockSpec(memory_space=pl.ANY)] + [vmem] * 8,
        out_specs=vmem,
        scratch_shapes=[
            pltpu.VMEM((chunks, s_dev, block, channels), jnp.bfloat16),
            pltpu.VMEM((channels, 2 * LANES), jnp.bfloat16),
            pltpu.VMEM((s_dev * block, LANES), jnp.float32),
            pltpu.VMEM((s_dev * block, LANES), jnp.float32),
            pltpu.VMEM((chunks, s_dev, wide), jnp.bfloat16),
            pltpu.VMEM((n_seq, s_dev, wide), jnp.bfloat16),
            pltpu.VMEM((chunks, n_seq, s_dev, wide), jnp.bfloat16),
            pltpu.VMEM((total // LANES, wide, LANES), jnp.float32),
            pltpu.VMEM((wide, total), jnp.bfloat16),
            pltpu.VMEM((wide, wide), jnp.float32),
            pltpu.VMEM((block * block, proj * proj), jnp.bfloat16),
            pltpu.VMEM((block * block, out_width), jnp.float32),
            pltpu.SemaphoreType.DMA((chunks,)),
            pltpu.SemaphoreType.DMA((chunks, n_seq)),
            pltpu.SemaphoreType.DMA((chunks, n_seq)),
            pltpu.SemaphoreType.DMA((chunks, n_seq)),
            pltpu.SemaphoreType.DMA((chunks, n_seq)),
            pltpu.SemaphoreType.DMA((chunks,)),
            pltpu.SemaphoreType.DMA((n_seq,)),
            pltpu.SemaphoreType.DMA((n_seq,)),
        ],
        compiler_params=pltpu.CompilerParams(
            collective_id=0, has_side_effects=True, vmem_limit_bytes=40 * 1024 * 1024
        ),
        name="outer_mean",
    )(
        alignment,
        ln_gain.reshape(1, -1),
        ln_bias.reshape(1, -1),
        w_left,
        bias_left.reshape(1, -1),
        w_right,
        bias_right.reshape(1, -1),
        w_out,
        bias_out.reshape(1, -1),
    )


def solution(mesh):
    return jax.shard_map(
        functools.partial(shards, mesh.shape["seq"], mesh.shape["res"]),
        mesh=mesh,
        in_specs=(P(("group", "seq"), "res", None), P(), P(), P(), P(), P(), P(), P(), P()),
        out_specs=P(("group", "seq"), "res", None),
        check_vma=False,
    )
```

```python
import functools
import math

import jax
import jax.numpy as jnp
from jax import lax
from jax.experimental import pallas as pl
from jax.experimental.pallas import tpu as pltpu
from jax.sharding import PartitionSpec as P

MESH = pl.DeviceIdType.MESH
LANES = 128


def normalize(alignment, ln_gain, ln_bias):
    values = alignment.astype(jnp.float32)
    center = jnp.mean(values, axis=-1, keepdims=True)
    spread = jnp.mean(jnp.square(values - center), axis=-1, keepdims=True)
    return ((values - center) * lax.rsqrt(spread + 1e-05) * ln_gain + ln_bias).astype(jnp.bfloat16)


def project(normed, weight, offset):
    flattened = normed.reshape(-1, normed.shape[-1])
    return (jnp.dot(flattened, weight, preferred_element_type=jnp.float32) + offset).astype(
        jnp.bfloat16
    )


def pair_tile(left_rows, right_rows, weight_cube, rows_here):
    sequences = left_rows.shape[0]
    proj_width = weight_cube.shape[0]
    height = math.gcd(rows_here, 16)
    left_blocks = left_rows.reshape(sequences, rows_here // height, height, proj_width).transpose(
        1, 0, 2, 3
    )
    right_cube = right_rows.reshape(sequences, -1, proj_width)

    def one_block(left_block):
        outers = jnp.einsum(
            "sic,sje->icej", left_block, right_cube, preferred_element_type=jnp.float32
        ).astype(jnp.bfloat16)
        return jnp.einsum("icej,ceo->ijo", outers, weight_cube, preferred_element_type=jnp.float32)

    pieces = lax.map(one_block, left_blocks)
    return pieces.reshape(rows_here, right_cube.shape[1], weight_cube.shape[2])


def plain(alignment, ln_gain, ln_bias, w_left, bias_left, w_right, bias_right, w_out, bias_out):
    sequences = alignment.shape[0]
    residues = alignment.shape[1]
    proj_width = w_left.shape[1]
    out_width = w_out.shape[1]
    normed = normalize(alignment, ln_gain, ln_bias)
    left_rows = project(normed, w_left, bias_left).reshape(sequences, residues * proj_width)
    right_rows = project(normed, w_right, bias_right).reshape(sequences, residues * proj_width)
    weight_cube = w_out.reshape(proj_width, proj_width, out_width)
    columns = lax.all_gather(left_rows, "res", axis=1, tiled=True)
    width_all = columns.shape[1] // proj_width
    devices_seq = lax.axis_size("seq")
    kept_rows = width_all // devices_seq
    summed = lax.psum_scatter(
        pair_tile(columns, right_rows, weight_cube, lax.axis_size("seq") * kept_rows),
        "seq",
        scatter_dimension=0,
        tiled=True,
    )
    return (summed / (sequences * devices_seq) + bias_out).astype(jnp.bfloat16)


def fused_kernel(
    dims,
    a_hbm, gain_hbm, beta_hbm, wl_hbm, bl_hbm, wr_hbm, br_hbm, w_hbm, bo_hbm,
    out_ref,
    gain_ref, beta_ref, wl_ref, bl_ref, wr_ref, br_ref, w_ref, bo_ref,
    a_buf, w_tiled, proj_l, proj_r, l_send, l_all, r_all, lt_f32, lt, outer, lhs, outs,
    load_sem, small_sem, r_recv, up_sem, down_sem, side_sem, l_send_sem, l_recv, core_send,
):
    n_seq, n_res, depth, s_dev, block, chunks, width, channels, proj = dims
    pack = LANES // proj
    quads = block // pack
    total = n_seq * s_dev
    p = lax.axis_index("seq")
    r = lax.axis_index("res")
    rows = n_seq // depth
    z = p // depth
    y = p % depth
    side = z * depth + (depth - 1 - y)

    small = []
    for n, (hbm, ref) in enumerate(
        [
            (gain_hbm, gain_ref),
            (beta_hbm, beta_ref),
            (wl_hbm, wl_ref),
            (bl_hbm, bl_ref),
            (wr_hbm, wr_ref),
            (br_hbm, br_ref),
            (w_hbm, w_ref),
            (bo_hbm, bo_ref),
        ]
    ):
        small.append(pltpu.make_async_copy(hbm, ref, small_sem.at[n]))
    for load in small[:6]:
        load.start()
    loads = []
    for k in range(chunks):
        load = pltpu.make_async_copy(
            a_hbm.at[:, pl.ds(k * block, block), :], a_buf.at[k], load_sem.at[k]
        )
        load.start()
        loads.append(load)
    for load in small[6:]:
        load.start()

    barrier = pltpu.get_barrier_semaphore()
    for d in range(1, n_seq):
        pl.semaphore_signal(
            barrier, inc=1, device_id={"seq": lax.rem(p + d, n_seq)}, device_id_type=MESH
        )
    pl.semaphore_signal(barrier, inc=1, device_id={"res": 1 - r}, device_id_type=MESH)

    def tile4(v):
        return jnp.concatenate([v] * pack, axis=1)

    for load in small[:6]:
        load.wait()
    both = [wl_ref[...].astype(jnp.float32)] * pack + [wr_ref[...].astype(jnp.float32)] * pack
    w_tiled[...] = jnp.transpose(jnp.concatenate(both, axis=0)).astype(jnp.bfloat16)
    bias_l = tile4(bl_ref[...])
    bias_r = tile4(br_ref[...])
    gain = gain_ref[...]
    beta = beta_ref[...]
    lane = lax.broadcasted_iota(jnp.int32, (s_dev, LANES), 1) // proj

    def copy_r(k, slot, sem, target):
        return pltpu.make_async_remote_copy(
            src_ref=r_all.at[k, slot],
            dst_ref=r_all.at[k, slot],
            send_sem=sem.at[k, slot],
            recv_sem=r_recv.at[k, slot],
            device_id={"seq": target},
            device_id_type=MESH,
        )

    def copy_up(k, slot):
        return copy_r(k, slot, up_sem, p + depth)

    def copy_down(k, slot):
        return copy_r(k, slot, down_sem, p - depth)

    def copy_side(k, slot):
        return copy_r(k, slot, side_sem, side)

    def copy_l(k):
        return pltpu.make_async_remote_copy(
            src_ref=l_send.at[k],
            dst_ref=l_all.at[p],
            send_sem=l_send_sem.at[k],
            recv_sem=l_recv.at[p],
            device_id={"seq": r * chunks + k},
            device_id_type=MESH,
        )

    def copy_core(slot):
        return pltpu.make_async_remote_copy(
            src_ref=l_all.at[slot],
            dst_ref=l_all.at[slot],
            send_sem=core_send.at[slot],
            recv_sem=l_recv.at[slot],
            device_id={"res": 1 - r},
            device_id_type=MESH,
        )

    def hop(k, d):
        @pl.when(z - d >= 0)
        def _():
            slot = p - d * depth
            copy_down(k, slot).wait_recv()

            @pl.when(z + 1 < rows)
            def _():
                copy_up(k, slot).start()

            copy_side(k, slot).start()

        @pl.when(z + d < rows)
        def _():
            slot = p + d * depth
            copy_down(k, slot).wait_recv()

            @pl.when(z > 0)
            def _():
                copy_down(k, slot).start()

            copy_side(k, slot).start()

    def wave(t):
        for d in range(1, rows):
            if 0 <= t - d < chunks:
                hop(t - d, d)

    seqs = 16
    for k in range(chunks):
        loads[k].wait()

        def norm_step(t, carry, k=k):
            values = a_buf[k, pl.ds(t * seqs, seqs)].reshape(seqs * block, channels)
            values = values.astype(jnp.float32)
            center = jnp.mean(values, axis=-1, keepdims=True)
            values = values - center
            spread = jnp.mean(jnp.square(values), axis=-1, keepdims=True)
            normed = (values * lax.rsqrt(spread + 1e-05) * gain + beta).astype(jnp.bfloat16)
            result = jnp.dot(normed, w_tiled[...], preferred_element_type=jnp.float32)
            here = pl.ds(t * (seqs * block), seqs * block)
            proj_l[here, :] = result[:, :LANES] + bias_l
            proj_r[here, :] = result[:, LANES:] + bias_r
            return carry

        lax.fori_loop(0, s_dev // seqs, norm_step, 0)

        for q in range(quads):
            columns = slice(q * LANES, (q + 1) * LANES)

            def merge(ref):
                merged = ref[pl.ds(q * pack, s_dev, stride=block), :]
                for m in range(1, pack):
                    merged = jnp.where(
                        lane == m, ref[pl.ds(q * pack + m, s_dev, stride=block), :], merged
                    )
                return merged.astype(jnp.bfloat16)

            r_all[k, p, :, columns] = merge(proj_r)
            l_send[k, :, columns] = merge(proj_l)

        if k == 0:
            pl.semaphore_wait(barrier, n_seq)

        @pl.when(z + 1 < rows)
        def _():
            copy_up(k, p).start()

        @pl.when(z > 0)
        def _():
            copy_down(k, p).start()

        copy_side(k, p).start()

        @pl.when(r * chunks + k != p)
        def _():
            copy_l(k).start()

        @pl.when(r * chunks + k == p)
        def _():
            l_all[p] = l_send[k]

        wave(k)

    def gather_left():
        owner = p // chunks == r
        for d in range(n_seq):
            slot = lax.rem(p + d, n_seq)

            @pl.when(owner)
            def _():
                if d > 0:
                    copy_core(slot).wait_recv()
                copy_core(slot).start()

            @pl.when(jnp.logical_not(owner))
            def _():
                copy_core(slot).wait_recv()

        left = l_all[...].reshape(total, block * proj)
        for t in range(total // LANES):
            lt_f32[t] = jnp.transpose(left[t * LANES : (t + 1) * LANES].astype(jnp.float32))
            for c in range(proj):
                lt[c * block : (c + 1) * block, t * LANES : (t + 1) * LANES] = lt_f32[
                    t, pl.ds(c, block, stride=proj), :
                ].astype(jnp.bfloat16)

    high = (lax.broadcasted_iota(jnp.int32, (block, LANES), 1) // (2 * proj)) == 1
    odd = ((lax.broadcasted_iota(jnp.int32, (block, LANES), 1) // proj) % 2) == 1

    def compute(k):
        for zz in range(rows):
            copy_side(k, zz * depth + (depth - 1 - y)).wait_recv()
        right = r_all[k].reshape(total, block * proj)
        outer[...] = jnp.dot(lt[...], right, preferred_element_type=jnp.float32)

        def regroup(cq, carry):
            for jq in range(quads):
                v = [
                    outer[pl.ds((cq * pack + m) * block, block), jq * LANES : (jq + 1) * LANES]
                    for m in range(pack)
                ]
                a0 = jnp.where(high, pltpu.roll(v[2], 2 * proj, 1), v[0])
                a2 = jnp.where(high, v[2], pltpu.roll(v[0], 2 * proj, 1))
                a1 = jnp.where(high, pltpu.roll(v[3], 2 * proj, 1), v[1])
                a3 = jnp.where(high, v[3], pltpu.roll(v[1], 2 * proj, 1))
                t = [
                    jnp.where(odd, pltpu.roll(a1, proj, 1), a0),
                    jnp.where(odd, a1, pltpu.roll(a0, 3 * proj, 1)),
                    jnp.where(odd, pltpu.roll(a3, proj, 1), a2),
                    jnp.where(odd, a3, pltpu.roll(a2, 3 * proj, 1)),
                ]
                for m in range(pack):
                    lhs[
                        (jq * pack + m) * block : (jq * pack + m + 1) * block,
                        pl.ds(pl.multiple_of(cq * LANES, LANES), LANES),
                    ] = t[m].astype(jnp.bfloat16)
            return carry

        lax.fori_loop(0, proj // pack, regroup, 0)
        outs[...] = (
            jnp.dot(lhs[...], w_ref[...], preferred_element_type=jnp.float32) * (1.0 / total)
            + bo_ref[...]
        )
        for i in range(block):
            out_ref[i, pl.ds(k * block, block), :] = outs[
                pl.ds(i, block, stride=block), :
            ].astype(jnp.bfloat16)

    wave(chunks)
    gather_left()
    done = chunks + 1
    for load in small[6:]:
        load.wait()
    for k in range(chunks):
        while done < chunks + rows - 1 and done - (rows - 1) <= k + 1:
            wave(done)
            done += 1
        compute(k)

    owner = p // chunks == r
    for k in range(chunks):
        @pl.when(r * chunks + k != p)
        def _():
            copy_l(k).wait_send()

        for zz in range(rows):
            slot = zz * depth + y
            copy_side(k, slot).wait_send()

            @pl.when(jnp.logical_and(zz <= z, z + 1 < rows))
            def _():
                copy_up(k, slot).wait_send()

            @pl.when(jnp.logical_and(zz >= z, z > 0))
            def _():
                copy_down(k, slot).wait_send()

    @pl.when(owner)
    def _():
        for slot in range(n_seq):
            copy_core(slot).wait_send()


def shards(n_seq, n_res, alignment, ln_gain, ln_bias, w_left, bias_left, w_right, bias_right, w_out, bias_out):
    s_dev, width, channels = alignment.shape
    proj = w_left.shape[1]
    out_width = w_out.shape[1]
    block = width * n_res // n_seq
    depth = 2
    fits = (
        n_res == 2
        and n_seq % depth == 0
        and block % 16 == 0
        and width % block == 0
        and proj * 4 == LANES
        and out_width == LANES
        and s_dev % 16 == 0
        and (n_seq * s_dev) % LANES == 0
    )
    if not fits:
        return plain(
            alignment, ln_gain, ln_bias, w_left, bias_left, w_right, bias_right, w_out, bias_out
        )
    chunks = width // block
    total = n_seq * s_dev
    dims = (n_seq, n_res, depth, s_dev, block, chunks, width, channels, proj)
    vmem = pl.BlockSpec(memory_space=pltpu.VMEM)
    wide = block * proj
    return pl.pallas_call(
        functools.partial(fused_kernel, dims),
        out_shape=jax.ShapeDtypeStruct((block, width, out_width), jnp.bfloat16),
        in_specs=[pl.BlockSpec(memory_space=pl.ANY)] * 9,
        out_specs=vmem,
        scratch_shapes=[
            pltpu.VMEM((1, channels), jnp.float32),
            pltpu.VMEM((1, channels), jnp.float32),
            pltpu.VMEM((proj, channels), jnp.bfloat16),
            pltpu.VMEM((1, proj), jnp.float32),
            pltpu.VMEM((proj, channels), jnp.bfloat16),
            pltpu.VMEM((1, proj), jnp.float32),
            pltpu.VMEM((proj * proj, out_width), jnp.bfloat16),
            pltpu.VMEM((1, out_width), jnp.float32),
            pltpu.VMEM((chunks, s_dev, block, channels), jnp.bfloat16),
            pltpu.VMEM((channels, 2 * LANES), jnp.bfloat16),
            pltpu.VMEM((s_dev * block, LANES), jnp.float32),
            pltpu.VMEM((s_dev * block, LANES), jnp.float32),
            pltpu.VMEM((chunks, s_dev, wide), jnp.bfloat16),
            pltpu.VMEM((n_seq, s_dev, wide), jnp.bfloat16),
            pltpu.VMEM((chunks, n_seq, s_dev, wide), jnp.bfloat16),
            pltpu.VMEM((total // LANES, wide, LANES), jnp.float32),
            pltpu.VMEM((wide, total), jnp.bfloat16),
            pltpu.VMEM((wide, wide), jnp.float32),
            pltpu.VMEM((block * block, proj * proj), jnp.bfloat16),
            pltpu.VMEM((block * block, out_width), jnp.float32),
            pltpu.SemaphoreType.DMA((chunks,)),
            pltpu.SemaphoreType.DMA((8,)),
            pltpu.SemaphoreType.DMA((chunks, n_seq)),
            pltpu.SemaphoreType.DMA((chunks, n_seq)),
            pltpu.SemaphoreType.DMA((chunks, n_seq)),
            pltpu.SemaphoreType.DMA((chunks, n_seq)),
            pltpu.SemaphoreType.DMA((chunks,)),
            pltpu.SemaphoreType.DMA((n_seq,)),
            pltpu.SemaphoreType.DMA((n_seq,)),
        ],
        compiler_params=pltpu.CompilerParams(
            collective_id=0, has_side_effects=True, vmem_limit_bytes=60 * 1024 * 1024
        ),
        name="outer_mean",
    )(
        alignment,
        ln_gain.reshape(1, -1),
        ln_bias.reshape(1, -1),
        w_left.T,
        bias_left.reshape(1, -1),
        w_right.T,
        bias_right.reshape(1, -1),
        w_out,
        bias_out.reshape(1, -1),
    )


def solution(mesh):
    return jax.shard_map(
        functools.partial(shards, mesh.shape["seq"], mesh.shape["res"]),
        mesh=mesh,
        in_specs=(P(("group", "seq"), "res", None), P(), P(), P(), P(), P(), P(), P(), P()),
        out_specs=P(("group", "seq"), "res", None),
        check_vma=False,
    )
```

```python
import functools
import math

import jax
import jax.numpy as jnp
from jax import lax
from jax.experimental import pallas as pl
from jax.experimental.pallas import tpu as pltpu
from jax.sharding import PartitionSpec as P

MESH = pl.DeviceIdType.MESH
LANES = 128


def normalize(alignment, ln_gain, ln_bias):
    values = alignment.astype(jnp.float32)
    center = jnp.mean(values, axis=-1, keepdims=True)
    spread = jnp.mean(jnp.square(values - center), axis=-1, keepdims=True)
    return ((values - center) * lax.rsqrt(spread + 1e-05) * ln_gain + ln_bias).astype(jnp.bfloat16)


def project(normed, weight, offset):
    flattened = normed.reshape(-1, normed.shape[-1])
    return (jnp.dot(flattened, weight, preferred_element_type=jnp.float32) + offset).astype(
        jnp.bfloat16
    )


def pair_tile(left_rows, right_rows, weight_cube, rows_here):
    sequences = left_rows.shape[0]
    proj_width = weight_cube.shape[0]
    height = math.gcd(rows_here, 16)
    left_blocks = left_rows.reshape(sequences, rows_here // height, height, proj_width).transpose(
        1, 0, 2, 3
    )
    right_cube = right_rows.reshape(sequences, -1, proj_width)

    def one_block(left_block):
        outers = jnp.einsum(
            "sic,sje->icej", left_block, right_cube, preferred_element_type=jnp.float32
        ).astype(jnp.bfloat16)
        return jnp.einsum("icej,ceo->ijo", outers, weight_cube, preferred_element_type=jnp.float32)

    pieces = lax.map(one_block, left_blocks)
    return pieces.reshape(rows_here, right_cube.shape[1], weight_cube.shape[2])


def plain(alignment, ln_gain, ln_bias, w_left, bias_left, w_right, bias_right, w_out, bias_out):
    sequences = alignment.shape[0]
    residues = alignment.shape[1]
    proj_width = w_left.shape[1]
    out_width = w_out.shape[1]
    normed = normalize(alignment, ln_gain, ln_bias)
    left_rows = project(normed, w_left, bias_left).reshape(sequences, residues * proj_width)
    right_rows = project(normed, w_right, bias_right).reshape(sequences, residues * proj_width)
    weight_cube = w_out.reshape(proj_width, proj_width, out_width)
    columns = lax.all_gather(left_rows, "res", axis=1, tiled=True)
    width_all = columns.shape[1] // proj_width
    devices_seq = lax.axis_size("seq")
    kept_rows = width_all // devices_seq
    summed = lax.psum_scatter(
        pair_tile(columns, right_rows, weight_cube, lax.axis_size("seq") * kept_rows),
        "seq",
        scatter_dimension=0,
        tiled=True,
    )
    return (summed / (sequences * devices_seq) + bias_out).astype(jnp.bfloat16)


def fused_kernel(
    dims,
    a_hbm, gain_hbm, beta_hbm, wl_hbm, bl_hbm, wr_hbm, br_hbm, w_hbm, bo_hbm,
    out_ref,
    gain_ref, beta_ref, wl_ref, bl_ref, wr_ref, br_ref, w_ref, bo_ref,
    a_buf, w_tiled, proj_l, proj_r, l_send, l_all, r_all, lt_f32, lt, outer, lhs, outs,
    load_sem, small_sem, r_recv, up_sem, down_sem, side_sem, l_send_sem, l_recv, core_send,
):
    n_seq, n_res, depth, s_dev, block, chunks, width, channels, proj = dims
    pack = LANES // proj
    quads = block // pack
    total = n_seq * s_dev
    p = lax.axis_index("seq")
    r = lax.axis_index("res")
    rows = n_seq // depth
    z = p // depth
    y = p % depth
    side = z * depth + (depth - 1 - y)

    small = []
    for n, (hbm, ref) in enumerate(
        [
            (gain_hbm, gain_ref),
            (beta_hbm, beta_ref),
            (wl_hbm, wl_ref),
            (bl_hbm, bl_ref),
            (wr_hbm, wr_ref),
            (br_hbm, br_ref),
            (w_hbm, w_ref),
            (bo_hbm, bo_ref),
        ]
    ):
        small.append(pltpu.make_async_copy(hbm, ref, small_sem.at[n]))
    for load in small[:6]:
        load.start()
    loads = []
    for k in range(chunks):
        load = pltpu.make_async_copy(
            a_hbm.at[:, pl.ds(k * block, block), :], a_buf.at[k], load_sem.at[k]
        )
        load.start()
        loads.append(load)
    for load in small[6:]:
        load.start()

    barrier = pltpu.get_barrier_semaphore()
    for d in range(1, n_seq):
        pl.semaphore_signal(
            barrier, inc=1, device_id={"seq": lax.rem(p + d, n_seq)}, device_id_type=MESH
        )
    pl.semaphore_signal(barrier, inc=1, device_id={"res": 1 - r}, device_id_type=MESH)

    def tile4(v):
        return jnp.concatenate([v] * pack, axis=1)

    for load in small[:6]:
        load.wait()
    both = [wl_ref[...].astype(jnp.float32)] * pack + [wr_ref[...].astype(jnp.float32)] * pack
    w_tiled[...] = jnp.transpose(jnp.concatenate(both, axis=0)).astype(jnp.bfloat16)
    bias_l = tile4(bl_ref[...])
    bias_r = tile4(br_ref[...])
    gain = gain_ref[...]
    beta = beta_ref[...]
    lane = lax.broadcasted_iota(jnp.int32, (s_dev, LANES), 1) // proj

    def copy_r(k, slot, sem, target):
        return pltpu.make_async_remote_copy(
            src_ref=r_all.at[k, slot],
            dst_ref=r_all.at[k, slot],
            send_sem=sem.at[k, slot],
            recv_sem=r_recv.at[k, slot],
            device_id={"seq": target},
            device_id_type=MESH,
        )

    def copy_up(k, slot):
        return copy_r(k, slot, up_sem, p + depth)

    def copy_down(k, slot):
        return copy_r(k, slot, down_sem, p - depth)

    def copy_side(k, slot):
        return copy_r(k, slot, side_sem, side)

    def copy_l(k):
        return pltpu.make_async_remote_copy(
            src_ref=l_send.at[k],
            dst_ref=l_all.at[p],
            send_sem=l_send_sem.at[k],
            recv_sem=l_recv.at[p],
            device_id={"seq": r * chunks + k},
            device_id_type=MESH,
        )

    def copy_core(slot):
        return pltpu.make_async_remote_copy(
            src_ref=l_all.at[slot],
            dst_ref=l_all.at[slot],
            send_sem=core_send.at[slot],
            recv_sem=l_recv.at[slot],
            device_id={"res": 1 - r},
            device_id_type=MESH,
        )

    def hop(k, d):
        @pl.when(z - d >= 0)
        def _():
            slot = p - d * depth
            copy_down(k, slot).wait_recv()

            @pl.when(z + 1 < rows)
            def _():
                copy_up(k, slot).start()

            copy_side(k, slot).start()

        @pl.when(z + d < rows)
        def _():
            slot = p + d * depth
            copy_down(k, slot).wait_recv()

            @pl.when(z > 0)
            def _():
                copy_down(k, slot).start()

            copy_side(k, slot).start()

    def wave(t):
        for d in range(1, rows):
            if 0 <= t - d < chunks:
                hop(t - d, d)

    seqs = 16
    for k in range(chunks):
        loads[k].wait()

        def norm_step(t, carry, k=k):
            values = a_buf[k, pl.ds(t * seqs, seqs)].reshape(seqs * block, channels)
            values = values.astype(jnp.float32)
            center = jnp.mean(values, axis=-1, keepdims=True)
            values = values - center
            spread = jnp.mean(jnp.square(values), axis=-1, keepdims=True)
            normed = (values * lax.rsqrt(spread + 1e-05) * gain + beta).astype(jnp.bfloat16)
            result = jnp.dot(normed, w_tiled[...], preferred_element_type=jnp.float32)
            here = pl.ds(t * (seqs * block), seqs * block)
            proj_l[here, :] = result[:, :LANES] + bias_l
            proj_r[here, :] = result[:, LANES:] + bias_r
            return carry

        lax.fori_loop(0, s_dev // seqs, norm_step, 0, unroll=True)

        for q in range(quads):
            columns = slice(q * LANES, (q + 1) * LANES)

            def merge(ref):
                merged = ref[pl.ds(q * pack, s_dev, stride=block), :]
                for m in range(1, pack):
                    merged = jnp.where(
                        lane == m, ref[pl.ds(q * pack + m, s_dev, stride=block), :], merged
                    )
                return merged.astype(jnp.bfloat16)

            r_all[k, p, :, columns] = merge(proj_r)
            l_send[k, :, columns] = merge(proj_l)

        if k == 0:
            pl.semaphore_wait(barrier, n_seq)

        copy_side(k, p).start()

        @pl.when(z + 1 < rows)
        def _():
            copy_up(k, p).start()

        @pl.when(z > 0)
        def _():
            copy_down(k, p).start()

        @pl.when(r * chunks + k != p)
        def _():
            copy_l(k).start()

        @pl.when(r * chunks + k == p)
        def _():
            l_all[p] = l_send[k]

        wave(k)

    def gather_left():
        owner = p // chunks == r
        for d in range(n_seq):
            slot = lax.rem(p + d, n_seq)

            @pl.when(owner)
            def _():
                if d > 0:
                    copy_core(slot).wait_recv()
                copy_core(slot).start()

            @pl.when(jnp.logical_not(owner))
            def _():
                copy_core(slot).wait_recv()

        left = l_all[...].reshape(total, block * proj)
        for t in range(total // LANES):
            lt_f32[t] = jnp.transpose(left[t * LANES : (t + 1) * LANES].astype(jnp.float32))
            for c in range(proj):
                lt[c * block : (c + 1) * block, t * LANES : (t + 1) * LANES] = lt_f32[
                    t, pl.ds(c, block, stride=proj), :
                ].astype(jnp.bfloat16)

    high = (lax.broadcasted_iota(jnp.int32, (block, LANES), 1) // (2 * proj)) == 1
    odd = ((lax.broadcasted_iota(jnp.int32, (block, LANES), 1) // proj) % 2) == 1

    def compute(k):
        for zz in range(rows):
            copy_side(k, zz * depth + (depth - 1 - y)).wait_recv()
        right = r_all[k].reshape(total, block * proj)
        outer[...] = jnp.dot(lt[...], right, preferred_element_type=jnp.float32)

        def regroup(cq, carry):
            for jq in range(quads):
                v = [
                    outer[pl.ds((cq * pack + m) * block, block), jq * LANES : (jq + 1) * LANES]
                    for m in range(pack)
                ]
                a0 = jnp.where(high, pltpu.roll(v[2], 2 * proj, 1), v[0])
                a2 = jnp.where(high, v[2], pltpu.roll(v[0], 2 * proj, 1))
                a1 = jnp.where(high, pltpu.roll(v[3], 2 * proj, 1), v[1])
                a3 = jnp.where(high, v[3], pltpu.roll(v[1], 2 * proj, 1))
                t = [
                    jnp.where(odd, pltpu.roll(a1, proj, 1), a0),
                    jnp.where(odd, a1, pltpu.roll(a0, 3 * proj, 1)),
                    jnp.where(odd, pltpu.roll(a3, proj, 1), a2),
                    jnp.where(odd, a3, pltpu.roll(a2, 3 * proj, 1)),
                ]
                for m in range(pack):
                    lhs[
                        (jq * pack + m) * block : (jq * pack + m + 1) * block,
                        pl.ds(pl.multiple_of(cq * LANES, LANES), LANES),
                    ] = t[m].astype(jnp.bfloat16)
            return carry

        lax.fori_loop(0, proj // pack, regroup, 0, unroll=True)
        outs[...] = (
            jnp.dot(lhs[...], w_ref[...], preferred_element_type=jnp.float32) * (1.0 / total)
            + bo_ref[...]
        )
        for i in range(block):
            out_ref[i, pl.ds(k * block, block), :] = outs[
                pl.ds(i, block, stride=block), :
            ].astype(jnp.bfloat16)

    wave(chunks)
    gather_left()
    done = chunks + 1
    for load in small[6:]:
        load.wait()
    for k in range(chunks):
        while done < chunks + rows - 1 and done - (rows - 1) <= k + 2:
            wave(done)
            done += 1
        compute(k)

    owner = p // chunks == r
    for k in range(chunks):
        @pl.when(r * chunks + k != p)
        def _():
            copy_l(k).wait_send()

        for zz in range(rows):
            slot = zz * depth + y
            copy_side(k, slot).wait_send()

            @pl.when(jnp.logical_and(zz <= z, z + 1 < rows))
            def _():
                copy_up(k, slot).wait_send()

            @pl.when(jnp.logical_and(zz >= z, z > 0))
            def _():
                copy_down(k, slot).wait_send()

    @pl.when(owner)
    def _():
        for slot in range(n_seq):
            copy_core(slot).wait_send()


def shards(n_seq, n_res, alignment, ln_gain, ln_bias, w_left, bias_left, w_right, bias_right, w_out, bias_out):
    s_dev, width, channels = alignment.shape
    proj = w_left.shape[1]
    out_width = w_out.shape[1]
    block = width * n_res // n_seq
    depth = 2
    fits = (
        n_res == 2
        and n_seq % depth == 0
        and block % 16 == 0
        and width % block == 0
        and proj * 4 == LANES
        and out_width == LANES
        and s_dev % 16 == 0
        and (n_seq * s_dev) % LANES == 0
    )
    if not fits:
        return plain(
            alignment, ln_gain, ln_bias, w_left, bias_left, w_right, bias_right, w_out, bias_out
        )
    chunks = width // block
    total = n_seq * s_dev
    dims = (n_seq, n_res, depth, s_dev, block, chunks, width, channels, proj)
    vmem = pl.BlockSpec(memory_space=pltpu.VMEM)
    wide = block * proj
    return pl.pallas_call(
        functools.partial(fused_kernel, dims),
        out_shape=jax.ShapeDtypeStruct((block, width, out_width), jnp.bfloat16),
        in_specs=[pl.BlockSpec(memory_space=pl.ANY)] * 9,
        out_specs=vmem,
        scratch_shapes=[
            pltpu.VMEM((1, channels), jnp.float32),
            pltpu.VMEM((1, channels), jnp.float32),
            pltpu.VMEM((proj, channels), jnp.bfloat16),
            pltpu.VMEM((1, proj), jnp.float32),
            pltpu.VMEM((proj, channels), jnp.bfloat16),
            pltpu.VMEM((1, proj), jnp.float32),
            pltpu.VMEM((proj * proj, out_width), jnp.bfloat16),
            pltpu.VMEM((1, out_width), jnp.float32),
            pltpu.VMEM((chunks, s_dev, block, channels), jnp.bfloat16),
            pltpu.VMEM((channels, 2 * LANES), jnp.bfloat16),
            pltpu.VMEM((s_dev * block, LANES), jnp.float32),
            pltpu.VMEM((s_dev * block, LANES), jnp.float32),
            pltpu.VMEM((chunks, s_dev, wide), jnp.bfloat16),
            pltpu.VMEM((n_seq, s_dev, wide), jnp.bfloat16),
            pltpu.VMEM((chunks, n_seq, s_dev, wide), jnp.bfloat16),
            pltpu.VMEM((total // LANES, wide, LANES), jnp.float32),
            pltpu.VMEM((wide, total), jnp.bfloat16),
            pltpu.VMEM((wide, wide), jnp.float32),
            pltpu.VMEM((block * block, proj * proj), jnp.bfloat16),
            pltpu.VMEM((block * block, out_width), jnp.float32),
            pltpu.SemaphoreType.DMA((chunks,)),
            pltpu.SemaphoreType.DMA((8,)),
            pltpu.SemaphoreType.DMA((chunks, n_seq)),
            pltpu.SemaphoreType.DMA((chunks, n_seq)),
            pltpu.SemaphoreType.DMA((chunks, n_seq)),
            pltpu.SemaphoreType.DMA((chunks, n_seq)),
            pltpu.SemaphoreType.DMA((chunks,)),
            pltpu.SemaphoreType.DMA((n_seq,)),
            pltpu.SemaphoreType.DMA((n_seq,)),
        ],
        compiler_params=pltpu.CompilerParams(
            collective_id=0, has_side_effects=True, vmem_limit_bytes=60 * 1024 * 1024
        ),
        name="outer_mean",
    )(
        alignment,
        ln_gain.reshape(1, -1),
        ln_bias.reshape(1, -1),
        w_left.T,
        bias_left.reshape(1, -1),
        w_right.T,
        bias_right.reshape(1, -1),
        w_out,
        bias_out.reshape(1, -1),
    )


def solution(mesh):
    return jax.shard_map(
        functools.partial(shards, mesh.shape["seq"], mesh.shape["res"]),
        mesh=mesh,
        in_specs=(P(("group", "seq"), "res", None), P(), P(), P(), P(), P(), P(), P(), P()),
        out_specs=P(("group", "seq"), "res", None),
        check_vma=False,
    )
```
